768 devices in a mesh: loop: 96 (over y, x, z_lo), rep: 8 (over z_hi, core).
Axes of the slice: x: 4, y: 8, z: 12 (z_hi: 4, z_lo: 3; z = z_hi * 3 + z_lo), core: 2. Of those that a mesh axis runs over, the one named last changes fastest.
Arguments:
- features: bfloat16 [98304, 256], P(('loop', 'rep')), may hold values from -6 to 6
- kernel_tiles: bfloat16 [768, 128, 128, 128], P(('loop', 'rep')), may hold values from -0.125 to 0.125
- row_starts: int32 [768, 9], P(('loop', 'rep')), may hold values from 0 to 128, as said below
- column_block: int32 [768, 128], P(('loop', 'rep')), may hold values from 0 to 767, as said below
- self_weight: bfloat16 [256, 256], replicated, may hold values from -0.375 to 0.375
- kernel_weight: bfloat16 [256, 256], replicated, may hold values from -0.375 to 0.375
- cotangent: bfloat16 [98304, 256], P(('loop', 'rep')), may hold values from -28 to 28
Outputs:
- layer_out: bfloat16 [98304, 256], P(('loop', 'rep'))
- feature_grad: bfloat16 [98304, 256], P(('loop', 'rep'))
- weight_grads: float32 [2, 256, 256], replicated
The draws below stay inside these ranges and needn't reach their ends.
Inputs may be any that keep to these rules, and one draw needn't show every extreme that they name: `row_starts`: in each row, the entries start at 0 and never fall; the last is the group's live slot count, at least 32, and some group has 128 live slots. column_block[d, s] // 8 differs from d // 8 by at most 1; the live slots of one group hold distinct pairs of row block and column block.
All inputs are finite; a program needn't handle non-finite values.
Results may differ from the reference program's by a relative error of at most 0.025.
Values may be sent and summed in bfloat16 or wider, within the bound.
A program may use at most 64 MiB of HBM per device.

```python
import math
import jax
import jax.numpy as jnp
from jax import lax

FEAT = 256
TILE = 128
SLOTS = 128
REACH = 1
GROUPS = 768
NODES = 98304
N_LOOP = 96
N_REP = 8


def slot_plan(key):
    groups = N_LOOP * N_REP
    span = 2 * REACH + 1
    across = span * N_REP
    candidates = N_REP * across
    key = jax.random.fold_in(key, 101)
    key_total, key_full, key_rank = jax.random.split(key, 3)
    totals = jax.random.randint(key_total, (groups,), SLOTS // 4, SLOTS + 1)
    fullest = jax.random.randint(key_full, (), 0, groups)
    totals = jnp.where(jnp.arange(groups) == fullest, SLOTS, totals).astype(jnp.int32)
    rank_keys = jax.random.split(key_rank, groups)
    ranks = jax.vmap(lambda one: jax.random.permutation(one, candidates))(rank_keys).astype(jnp.int32)
    places = jnp.arange(candidates, dtype=jnp.int32)
    place_local = places % across
    band_ids = jnp.arange(groups, dtype=jnp.int32) // N_REP
    place_band = band_ids[:, None] - REACH + (place_local // N_REP)[None, :]
    invalid = ((place_band < 0) | (place_band > N_LOOP - 1)).astype(jnp.int32)
    score = ranks + invalid * candidates
    chosen = jnp.argsort(score, axis=1, stable=True)[:, :SLOTS].astype(jnp.int32)
    slot_ids = jnp.arange(SLOTS, dtype=jnp.int32)
    live = (slot_ids[None, :] < totals[:, None]).astype(jnp.int32)
    chosen_row = chosen // across
    order_key = (chosen_row * live + N_REP * (1 - live)) * candidates + chosen
    order = jnp.argsort(order_key, axis=1, stable=True)
    chosen = jnp.take_along_axis(chosen, order, axis=1).astype(jnp.int32)
    chosen_row = chosen // across
    chosen_local = chosen % across
    column_block = (band_ids[:, None] - REACH) * N_REP + chosen_local
    bounds = jnp.arange(N_REP, dtype=jnp.int32)
    below = (chosen_row[:, :, None] < bounds[None, None, :]).astype(jnp.int32) * live[:, :, None]
    starts = jnp.sum(below, axis=1).astype(jnp.int32)
    row_starts = jnp.concatenate([starts, totals[:, None]], axis=1).astype(jnp.int32)
    return (row_starts, column_block.astype(jnp.int32))


def draw_row_starts(key, part):
    return slot_plan(key)[0]


def draw_column_block(key, part):
    return slot_plan(key)[1]


def draw_cotangent(key, part):
    key = jax.random.fold_in(key, 7)
    key_scale, key_heavy, key_value = jax.random.split(key, 3)
    block_count = NODES // TILE
    logs = jax.random.uniform(key_scale, (block_count,), jnp.float32, 0.0, jnp.log(16.0))
    scales = jnp.exp(logs)
    heavy = jax.random.randint(key_heavy, (), 0, block_count)
    scales = jnp.where(jnp.arange(block_count) == heavy, 32.0, scales) / 7.0
    values = jnp.clip(jax.random.normal(key_value, (block_count, TILE, FEAT), jnp.float32), -6.0, 6.0)
    return (values * scales[:, None, None]).reshape(NODES, FEAT).astype(jnp.bfloat16)


def level_of(own_key, shape, cuts, least, high):
    loudness = 1.0
    for axis_at, shards_of in cuts:
        draws = jax.random.uniform(jax.random.fold_in(jax.random.fold_in(own_key, 6), axis_at), (shards_of,), jnp.float32, least / len(cuts), high / len(cuts))
        loudness = loudness * jnp.repeat(jnp.exp(draws), shape[axis_at] // shards_of).reshape((-1,) + (1,) * (len(shape) - 1 - axis_at))
    return loudness


def bell_draw(stream_key, shape, width, reach, cuts=(), held_as=jnp.bfloat16):
    level = level_of(stream_key, shape, cuts, -0.22, 0.18) if cuts else 1.0
    drawn = jax.random.normal(stream_key, shape, jnp.float32) * width * level
    return jnp.minimum(jnp.maximum(drawn, -reach), reach).astype(held_as)


def setup_inputs(seed: int = 0) -> dict:
    key_list = jax.random.split(jax.random.key(seed), 8)
    features = bell_draw(key_list[0], (NODES, FEAT), 1.0, 6.0, ((0, 768),))
    kernel_tiles = bell_draw(key_list[1], (GROUPS, SLOTS, TILE, TILE), (TILE * SLOTS // N_REP) ** -0.5, 0.125, ((0, 768),))
    row_starts = draw_row_starts(jax.random.fold_in(key_list[7], 71), 0)
    column_block = draw_column_block(jax.random.fold_in(key_list[7], 71), 0)
    self_weight = bell_draw(key_list[4], (FEAT, FEAT), FEAT ** -0.5, 0.375)
    kernel_weight = bell_draw(key_list[5], (FEAT, FEAT), FEAT ** -0.5, 0.375)
    cotangent = draw_cotangent(jax.random.fold_in(key_list[7], 71), 0)
    return dict(features=features, kernel_tiles=kernel_tiles, row_starts=row_starts, column_block=column_block, self_weight=self_weight, kernel_weight=kernel_weight, cotangent=cotangent)


def slot_layout(starts, columns, device):
    slot_ids = jnp.arange(SLOTS, dtype=jnp.int32)
    interior = starts[1:N_REP]
    row_of = lax.optimization_barrier(jnp.sum((interior[None, :] <= slot_ids[:, None]).astype(jnp.int32), axis=1))
    live_mask = (slot_ids < starts[N_REP]).astype(jnp.float32)
    band_base = device // N_REP * N_REP
    return ((band_base + row_of).astype(jnp.int32), columns.astype(jnp.int32), live_mask)

def reference(features, kernel_tiles, row_starts, column_block, self_weight, kernel_weight, cotangent):
    groups = N_LOOP * N_REP
    blocks = features.reshape(groups, TILE, FEAT)
    device_ids = jnp.arange(groups, dtype=jnp.int32)

    def forward_step(running, device):
        row_blocks, col_blocks, live_mask = slot_layout(row_starts[device], column_block[device], device)
        near_rows = blocks[col_blocks].astype(jnp.float32)
        tile_block = kernel_tiles[device].astype(jnp.float32)
        products = jnp.einsum('sab,sbf->saf', tile_block, near_rows) * live_mask[:, None, None]
        return (running.at[row_blocks].add(products), None)
    kernel_sum = lax.scan(forward_step, jnp.zeros((groups, TILE, FEAT), jnp.float32), device_ids)[0]
    kernel_rows = kernel_sum.reshape(NODES, FEAT).astype(jnp.bfloat16)
    preact = jnp.dot(features, self_weight, preferred_element_type=jnp.float32) + jnp.dot(kernel_rows, kernel_weight, preferred_element_type=jnp.float32)
    activated, pullback = jax.vjp(jax.nn.gelu, preact)
    layer_out = activated.astype(jnp.bfloat16)
    grad_pre = pullback(cotangent.astype(jnp.float32))[0].astype(jnp.bfloat16)
    norm_scale = 1.0 / math.sqrt(NODES)
    grad_self = jnp.dot(features.T, grad_pre, preferred_element_type=jnp.float32)
    grad_kernel = jnp.dot(kernel_rows.T, grad_pre, preferred_element_type=jnp.float32)
    weight_grads = jnp.stack([grad_self, grad_kernel]) * norm_scale
    kernel_grad = jnp.dot(grad_pre, kernel_weight.T, preferred_element_type=jnp.float32).astype(jnp.bfloat16)
    grad_blocks = kernel_grad.reshape(groups, TILE, FEAT)

    def backward_step(running, device):
        row_blocks, col_blocks, live_mask = slot_layout(row_starts[device], column_block[device], device)
        left_rows = grad_blocks[row_blocks].astype(jnp.float32)
        tile_block = kernel_tiles[device].astype(jnp.float32)
        products = jnp.einsum('sab,saf->sbf', tile_block, left_rows) * live_mask[:, None, None]
        return (running.at[col_blocks].add(products), None)
    transposed = lax.scan(backward_step, jnp.zeros((groups, TILE, FEAT), jnp.float32), device_ids)[0]
    self_part = jnp.dot(grad_pre, self_weight.T, preferred_element_type=jnp.float32)
    feature_grad = (self_part + transposed.reshape(NODES, FEAT)).astype(jnp.bfloat16)
    return (layer_out, feature_grad, weight_grads)
```

```python
import math

import jax
import jax.numpy as jnp
from jax import lax
from jax.experimental import pallas as pl
from jax.experimental.pallas import tpu as pltpu
from jax.sharding import PartitionSpec as P

MESH = pl.DeviceIdType.MESH
BF16 = jnp.bfloat16
F32 = jnp.float32

NL, NX, NY, NH = 3, 4, 8, 4
BANDS = NL * NX * NY
REPS = NH * 2
TILE = 128
FEAT = 256
SLOTS = 128
SPAN = 3
ROWS = REPS * TILE


class Sems:
    def __init__(self):
        self.count = 0

    def take(self, number=1):
        first = self.count
        self.count += number
        return first


def sem_plan():
    sems = Sems()
    plan = {}
    for name, number in (
        ("a_h", 4), ("a_sib", 4), ("a_next", 4), ("a_prev", 4), ("a_sib_prev", 4), ("a_sib_next", 4),
        ("c_sib", 4), ("c_h", 4), ("e_h", 4), ("e_sib", 4),
        ("g_sib", 6), ("g_l", 4), ("g_h", 4),
        ("w_sib", 1), ("w_h", 4), ("w_y", 8), ("w_x", 4), ("w_l", 3),
        ("v_y", 8), ("v_h", 4), ("v_sib", 4),
    ):
        plan[name] = sems.take(number)
    return plan, sems.count


PLAN, N_SEMS = sem_plan()


def dot(a, b):
    return jnp.dot(a, b, preferred_element_type=F32)


def dot_nt(a, b):
    return lax.dot_general(a, b, (((1,), (1,)), ((), ())), preferred_element_type=F32)


def dot_tn(a, b):
    return lax.dot_general(a, b, (((0,), (0,)), ((), ())), preferred_element_type=F32)


def kernel(
    slot_ref, feat_ref, ws_ref, wk_ref, cot_ref, tiles_hbm,
    out_ref, fg_ref, wg_ref,
    tiles, a_mat, f_buf, p_acc, c_send, c_sib, c_chip, c_recv,
    g_t, r_own, r_send, r_sib, r_chip, r_l, r_hs, r_h,
    w_f32, w_send, w_sib, w2_send, w2_recv, w3_src, w3_recv, w4_all, w5_all, w6_all, w7_all,
    tile_sem, ssem, rsem,
):
    loop = lax.axis_index("loop")
    rep = lax.axis_index("rep")
    core = lax.rem(rep, 2)
    other = 1 - core
    h = lax.div(rep, 2)
    l = lax.rem(loop, NL)
    x = lax.rem(lax.div(loop, NL), NX)
    y = lax.div(loop, NL * NX)

    def turn(value, step, count):
        return lax.rem(value + (step % count), count)

    h_next = lax.rem(h + jnp.where(l == NL - 1, 1, 0), NH)
    h_prev = lax.rem(h + jnp.where(l == 0, NH - 1, 0), NH)
    sib_dev = (loop, h * 2 + other)
    next_dev = (lax.rem(loop + 1, BANDS), h_next * 2 + core)
    prev_dev = (lax.rem(loop + BANDS - 1, BANDS), h_prev * 2 + core)
    h_dev = {k: (loop, turn(h, k, NH) * 2 + core) for k in range(1, NH)}
    y_dev = {k: ((turn(y, k, NY) * NX + x) * NL + l, rep) for k in range(1, NY)}
    x_dev = {k: ((y * NX + turn(x, k, NX)) * NL + l, rep) for k in range(1, NX)}
    l_dev = {k: ((y * NX + x) * NL + turn(l, k, NL), rep) for k in range(1, NL)}

    started = []

    def copy(src, dst, name, index, device):
        at = PLAN[name] + index
        return pltpu.make_async_remote_copy(
            src_ref=src, dst_ref=dst, send_sem=ssem.at[at], recv_sem=rsem.at[at],
            device_id=device, device_id_type=MESH,
        )

    def send(src, dst, name, index, device):
        one = copy(src, dst, name, index, device)
        one.start()
        started.append(one)

    def arrived(landing, name, index, device):
        copy(landing, landing, name, index, device).wait_recv()

    tiles_in = [
        pltpu.make_async_copy(tiles_hbm.at[0, pl.ds(q * 32, 32)], tiles.at[pl.ds(q * 32, 32)], tile_sem.at[q])
        for q in range(4)
    ]
    for one in tiles_in:
        one.start()

    barrier = pltpu.get_barrier_semaphore()
    partners = [sib_dev, next_dev, prev_dev]
    for group in (h_dev, y_dev, x_dev, l_dev):
        partners.extend(group.values())
    for device in partners:
        pl.semaphore_signal(barrier, inc=1, device_id=device, device_id_type=MESH)
    pl.semaphore_wait(barrier, len(partners))

    mine = f_buf.at[1, core, h]
    for k in (2, 1, 3):
        send(feat_ref, mine, "a_h", k, h_dev[k])
    send(feat_ref, f_buf.at[0, core, h], "a_next", 0, next_dev)
    send(feat_ref, f_buf.at[2, core, h], "a_prev", 0, prev_dev)
    send(feat_ref, mine, "a_sib", 0, sib_dev)
    f_buf[1, core, h] = feat_ref[...]

    tiles[SLOTS] = jnp.zeros((TILE, TILE), BF16)
    for one in tiles_in:
        one.wait()

    def assemble(b, carry):
        row = pl.multiple_of(b * TILE, TILE)
        for c in range(SPAN * REPS):
            at = slot_ref[b, c]
            a_mat[c // 2, pl.ds(row, TILE), (c % 2) * TILE:(c % 2 + 1) * TILE] = tiles[at]
        return carry

    lax.fori_loop(0, REPS, assemble, 0)

    for k in (1, 3, 2):
        behind = turn(h, -k, NH)
        here = f_buf.at[1, core, behind]
        arrived(here, "a_h", k, h_dev[k])
        send(here, f_buf.at[0, core, behind], "a_next", k, next_dev)
        send(here, f_buf.at[2, core, behind], "a_prev", k, prev_dev)
        send(here, here, "a_sib", k, sib_dev)
    for k in range(NH):
        arrived(f_buf.at[1, other, turn(h, -k, NH)], "a_sib", k, sib_dev)

    def forward_part(j, m):
        rows = pl.ds(pl.multiple_of(m * 256, 256), 256)
        left = jnp.concatenate([a_mat[4 * j + n, rows, :] for n in range(4)], axis=1)
        return dot(left, f_buf[j].reshape(ROWS, FEAT))

    def forward_own(m, carry):
        p_acc[pl.ds(2 * m, 2)] = forward_part(1, m).reshape(2, TILE, FEAT)
        return carry

    lax.fori_loop(0, 4, forward_own, 0)
    self_part = dot(feat_ref[...], ws_ref[...])

    for k in (0, 1, 3, 2):
        before = f_buf.at[0, core, turn(h_prev, -k, NH)]
        arrived(before, "a_next", k, prev_dev)
        send(before, before, "a_sib_prev", k, sib_dev)
        after = f_buf.at[2, core, turn(h_next, -k, NH)]
        arrived(after, "a_prev", k, next_dev)
        send(after, after, "a_sib_next", k, sib_dev)
    for k in range(NH):
        arrived(f_buf.at[0, other, turn(h_prev, -k, NH)], "a_sib_prev", k, sib_dev)
        arrived(f_buf.at[2, other, turn(h_next, -k, NH)], "a_sib_next", k, sib_dev)

    def forward_rest(m):
        both = pl.ds(2 * m, 2)
        return p_acc[both] + (forward_part(0, m) + forward_part(2, m)).reshape(2, TILE, FEAT)

    def forward_sibling(t, carry):
        c_send[pl.ds(2 * t, 2)] = forward_rest(other * 2 + t).astype(BF16)
        return carry

    lax.fori_loop(0, 2, forward_sibling, 0)
    for k in (2, 1, 3, 0):
        send(c_send.at[turn(h, k, NH)], c_sib.at[k], "c_sib", k, sib_dev)

    def forward_mine(t, carry):
        m = core * 2 + t
        p_acc[pl.ds(2 * m, 2)] = forward_rest(m)
        return carry

    lax.fori_loop(0, 2, forward_mine, 0)
    for k in (2, 1, 3):
        arrived(c_sib.at[k], "c_sib", k, sib_dev)
        c_chip[k] = (p_acc[core * NH + turn(h, k, NH)] + c_sib[k].astype(F32)).astype(BF16)
        send(c_chip.at[k], c_recv.at[k], "c_h", k, h_dev[k])
    arrived(c_sib.at[0], "c_sib", 0, sib_dev)
    kernel_sum = p_acc[core * NH + h] + c_sib[0].astype(F32)
    for k in (1, 3, 2):
        arrived(c_recv.at[k], "c_h", k, h_dev[k])
        kernel_sum = kernel_sum + c_recv[k].astype(F32)
    kernel_rows = kernel_sum.astype(BF16)

    preact = self_part + dot(kernel_rows, wk_ref[...])
    root = math.sqrt(2.0 / math.pi)
    square = preact * preact
    bend = jnp.tanh(root * (preact + 0.044715 * (square * preact)))
    half = 0.5 * (1.0 + bend)
    out_ref[...] = (preact * half).astype(BF16)
    slope = half + 0.5 * preact * (1.0 - bend * bend) * (root * (1.0 + 3.0 * 0.044715 * square))
    grad_pre = (cot_ref[...].astype(F32) * slope).astype(BF16)

    g_t[core, h] = dot_nt(wk_ref[...], grad_pre).astype(BF16)
    mine = g_t.at[core, h]
    for k in (2, 1, 3):
        send(mine, mine, "e_h", k, h_dev[k])
    send(mine, mine, "e_sib", 0, sib_dev)

    w_f32[0] = dot_tn(feat_ref[...], grad_pre)
    w_f32[1] = dot_tn(kernel_rows, grad_pre)
    w_send[...] = w_f32[other].astype(BF16)
    send(w_send, w_sib, "w_sib", 0, sib_dev)
    returned = dot_nt(ws_ref[...], grad_pre)

    for k in (1, 3, 2):
        here = g_t.at[core, turn(h, -k, NH)]
        arrived(here, "e_h", k, h_dev[k])
        send(here, here, "e_sib", k, sib_dev)

    arrived(w_sib, "w_sib", 0, sib_dev)

    def chip_rows(block):
        rows = pl.ds(pl.multiple_of(block * 64, 64), 64)
        return w_f32[core, rows, :] + w_sib[rows, :].astype(F32)

    for k in range(1, NH):
        w2_send[k] = chip_rows(turn(h, k, NH)).astype(BF16)
        send(w2_send.at[k], w2_recv.at[k], "w_h", k, h_dev[k])

    for k in range(NH):
        arrived(g_t.at[other, turn(h, -k, NH)], "e_sib", k, sib_dev)

    def backward_part(j, n):
        left = jnp.concatenate([g_t[c, b] for c in range(2) for b in range(NH)], axis=1)
        return dot(left, a_mat[4 * j + n])

    def backward_band(j):
        def for_sibling(t, carry):
            part = backward_part(j, other * 2 + t).astype(BF16)
            r_send[j, 2 * t] = part[:, :TILE]
            r_send[j, 2 * t + 1] = part[:, TILE:]
            return carry

        lax.fori_loop(0, 2, for_sibling, 0)
        for t in range(2):
            two = pl.ds(2 * t, 2)
            send(r_send.at[j, two], r_sib.at[j, two], "g_sib", 2 * j + t, sib_dev)

        def for_me(t, carry):
            part = backward_part(j, core * 2 + t)
            r_own[j, 2 * t] = part[:, :TILE]
            r_own[j, 2 * t + 1] = part[:, TILE:]
            return carry

        lax.fori_loop(0, 2, for_me, 0)

    def to_beside(j, device):
        for t in range(2):
            two = pl.ds(2 * t, 2)
            arrived(r_sib.at[j, two], "g_sib", 2 * j + t, sib_dev)
            r_chip[j // 2, two] = (r_own[j, two] + r_sib[j, two].astype(F32)).astype(BF16)
            send(r_chip.at[j // 2, two], r_l.at[j // 2, two], "g_l", j + t, device)

    backward_band(0)
    backward_band(2)
    to_beside(0, prev_dev)
    to_beside(2, next_dev)

    for k in range(1, NH):
        arrived(w2_recv.at[k], "w_h", k, h_dev[k])
    part = chip_rows(h)
    for k in range(1, NH):
        part = part + w2_recv[k].astype(F32)
    for q in range(NY):
        w3_src[q] = part[(q // 2) * 16:(q // 2 + 1) * 16, (q % 2) * 128:(q % 2 + 1) * 128]
    for k in range(1, NY):
        send(w3_src.at[turn(y, k, NY)], w3_recv.at[k], "w_y", k, y_dev[k])

    backward_band(1)

    for k in range(1, NY):
        arrived(w3_recv.at[k], "w_y", k, y_dev[k])
    part = w3_src[y]
    for k in range(1, NY):
        part = part + w3_recv[k]
    w4_all[x] = part
    for k in range(1, NX):
        send(w4_all.at[x], w4_all.at[x], "w_x", k, x_dev[k])

    for t in range(2):
        arrived(r_sib.at[1, pl.ds(2 * t, 2)], "g_sib", 2 + t, sib_dev)
    r_own[1] = r_own[1] + r_sib[1].astype(F32)

    for k in range(1, NX):
        arrived(w4_all.at[turn(x, -k, NX)], "w_x", k, x_dev[k])
    part = w4_all[0]
    for q in range(1, NX):
        part = part + w4_all[q]
    w5_all[l] = part
    for k in range(1, NL):
        send(w5_all.at[l], w5_all.at[l], "w_l", k, l_dev[k])

    for t in range(2):
        two = pl.ds(2 * t, 2)
        arrived(r_l.at[0, two], "g_l", t, next_dev)
        arrived(r_l.at[1, two], "g_l", 2 + t, prev_dev)

    def summed(block):
        return r_own[1, block] + (r_l[0, block].astype(F32) + r_l[1, block].astype(F32))

    for k in (2, 1, 3):
        r_hs[k] = summed(turn(h, k, NH)).astype(BF16)
        send(r_hs.at[k], r_h.at[k], "g_h", k, h_dev[k])
    returned = returned + summed(h)

    for k in range(1, NL):
        arrived(w5_all.at[turn(l, -k, NL)], "w_l", k, l_dev[k])
    w6_all[y] = w5_all[0] + w5_all[1] + w5_all[2]
    for k in range(1, NY):
        send(w6_all.at[y], w6_all.at[y], "v_y", k, y_dev[k])
    for k in range(1, NY):
        arrived(w6_all.at[turn(y, -k, NY)], "v_y", k, y_dev[k])
    w7_all[core, h] = jnp.concatenate(
        [jnp.concatenate([w6_all[2 * q], w6_all[2 * q + 1]], axis=1) for q in range(NY // 2)], axis=0
    ).astype(BF16)
    mine = w7_all.at[core, h]
    for k in (2, 1, 3):
        send(mine, mine, "v_h", k, h_dev[k])
    send(mine, mine, "v_sib", 0, sib_dev)

    for k in (1, 3, 2):
        arrived(r_h.at[k], "g_h", k, h_dev[k])
        returned = returned + r_h[k].astype(F32)
    fg_ref[...] = returned.T.astype(BF16)

    for k in (1, 3, 2):
        here = w7_all.at[core, turn(h, -k, NH)]
        arrived(here, "v_h", k, h_dev[k])
        send(here, here, "v_sib", k, sib_dev)
    scale = 1.0 / math.sqrt(TILE * REPS * BANDS)
    for k in range(NH):
        arrived(w7_all.at[other, turn(h, -k, NH)], "v_sib", k, sib_dev)
    wg_ref[...] = w7_all[...].astype(F32).reshape(2, FEAT, FEAT) * scale

    for one in started:
        one.wait_send()


def scratch():
    return [
        pltpu.VMEM((SLOTS + 1, TILE, TILE), BF16),
        pltpu.VMEM((SPAN * REPS // 2, ROWS, 2 * TILE), BF16),
        pltpu.VMEM((SPAN, 2, NH, TILE, FEAT), BF16),
        pltpu.VMEM((REPS, TILE, FEAT), F32),
        pltpu.VMEM((NH, TILE, FEAT), BF16),
        pltpu.VMEM((NH, TILE, FEAT), BF16),
        pltpu.VMEM((NH, TILE, FEAT), BF16),
        pltpu.VMEM((NH, TILE, FEAT), BF16),
        pltpu.VMEM((2, NH, FEAT, TILE), BF16),
        pltpu.VMEM((SPAN, NH, FEAT, TILE), F32),
        pltpu.VMEM((SPAN, NH, FEAT, TILE), BF16),
        pltpu.VMEM((SPAN, NH, FEAT, TILE), BF16),
        pltpu.VMEM((2, NH, FEAT, TILE), BF16),
        pltpu.VMEM((2, NH, FEAT, TILE), BF16),
        pltpu.VMEM((NH, FEAT, TILE), BF16),
        pltpu.VMEM((NH, FEAT, TILE), BF16),
        pltpu.VMEM((2, FEAT, FEAT), F32),
        pltpu.VMEM((FEAT, FEAT), BF16),
        pltpu.VMEM((FEAT, FEAT), BF16),
        pltpu.VMEM((NH, 64, FEAT), BF16),
        pltpu.VMEM((NH, 64, FEAT), BF16),
        pltpu.VMEM((NY, 16, 128), F32),
        pltpu.VMEM((NY, 16, 128), F32),
        pltpu.VMEM((NX, 16, 128), F32),
        pltpu.VMEM((NL, 16, 128), F32),
        pltpu.VMEM((NY, 16, 128), F32),
        pltpu.VMEM((2, NH, 64, FEAT), BF16),
        pltpu.SemaphoreType.DMA((4,)),
        pltpu.SemaphoreType.DMA((N_SEMS,)),
        pltpu.SemaphoreType.DMA((N_SEMS,)),
    ]


def slot_table(row_starts, column_block):
    band = lax.axis_index("loop")
    slots = jnp.arange(SLOTS, dtype=jnp.int32)
    row = jnp.sum((row_starts[0, 1:REPS, None] <= slots[None, :]).astype(jnp.int32), axis=0)
    column = column_block[0] - (band - 1) * REPS
    side, within = column // REPS, column % REPS
    key = ((row % 2) * NH + row // 2) * (SPAN * REPS) + side * REPS + (within % 2) * NH + within // 2
    key = jnp.where(slots < row_starts[0, REPS], key, -1)
    places = jnp.arange(REPS * SPAN * REPS, dtype=jnp.int32)
    found = jnp.where(key[None, :] == places[:, None], slots[None, :] - SLOTS, 0)
    return (jnp.sum(found, axis=1) + SLOTS).reshape(REPS, SPAN * REPS)


def on_device(features, kernel_tiles, row_starts, column_block, self_weight, kernel_weight, cotangent):
    vmem = pl.BlockSpec(memory_space=pltpu.VMEM)
    return pl.pallas_call(
        kernel,
        out_shape=(
            jax.ShapeDtypeStruct((TILE, FEAT), BF16),
            jax.ShapeDtypeStruct((TILE, FEAT), BF16),
            jax.ShapeDtypeStruct((2, FEAT, FEAT), F32),
        ),
        in_specs=[pl.BlockSpec(memory_space=pltpu.SMEM), vmem, vmem, vmem, vmem, pl.BlockSpec(memory_space=pl.ANY)],
        out_specs=(vmem, vmem, vmem),
        scratch_shapes=scratch(),
        compiler_params=pltpu.CompilerParams(
            collective_id=0, has_side_effects=True, vmem_limit_bytes=48 * 1024 * 1024
        ),
    )(slot_table(row_starts, column_block), features, self_weight, kernel_weight, cotangent, kernel_tiles)


def solution(mesh):
    split = P(("loop", "rep"), None)
    return jax.shard_map(
        on_device,
        mesh=mesh,
        in_specs=(split, P(("loop", "rep"), None, None, None), split, split, P(), P(), split),
        out_specs=(split, split, P()),
        check_vma=False,
    )
```

```python
import math

import jax
import jax.numpy as jnp
from jax import lax
from jax.experimental import pallas as pl
from jax.experimental.pallas import tpu as pltpu
from jax.sharding import PartitionSpec as P

MESH = pl.DeviceIdType.MESH
BF16 = jnp.bfloat16
F32 = jnp.float32

NL, NX, NY, NH = 3, 4, 8, 4
BANDS = NL * NX * NY
REPS = NH * 2
TILE = 128
FEAT = 256
SLOTS = 128
SPAN = 3
ROWS = REPS * TILE


def sem_plan():
    plan, count = {}, 0
    for name, number in (
        ("a_h", 4), ("a_sib", 4), ("a_next", 4), ("a_prev", 4), ("a_sib_prev", 4), ("a_sib_next", 4),
        ("c_sib", 4), ("c_h", 4), ("e_h", 4), ("e_sib", 4),
        ("g_sib", 12), ("g_l", 8), ("g_h", 4),
        ("w_sib", 1), ("w_y", 8), ("w_x", 4), ("w_h", 4), ("w_l", 3),
        ("v_x", 4), ("v_y", 8), ("v_sib", 1),
    ):
        plan[name] = count
        count += number
    return plan, count


PLAN, N_SEMS = sem_plan()


def dot(a, b):
    return jnp.dot(a, b, preferred_element_type=F32)


def dot_nt(a, b):
    return lax.dot_general(a, b, (((1,), (1,)), ((), ())), preferred_element_type=F32)


def dot_tn(a, b):
    return lax.dot_general(a, b, (((0,), (0,)), ((), ())), preferred_element_type=F32)


def kernel(
    starts_ref, columns_ref, feat_hbm, ws_hbm, wk_hbm, cot_hbm, tiles_hbm,
    out_ref, fg_ref, wg_ref,
    feat_ref, ws_ref, wk_ref, cot_ref, table_v, table,
    tiles, a_mat, f_buf, p_acc, c_send, c_sib, c_chip, c_recv,
    g_t, r_acc, r_own, r_send, r_sib, r_chip, r_l, r_hs, r_h,
    w_f32, w_send, w_sib, wy_send, wy_recv, wx_send, wx_recv, wh_all, wl_all, vx_all, vy_all, v_mat,
    local_sem, ssem, rsem,
):
    loop = lax.axis_index("loop")
    rep = lax.axis_index("rep")
    core = lax.rem(rep, 2)
    other = 1 - core
    h = lax.div(rep, 2)
    l = lax.rem(loop, NL)
    x = lax.rem(lax.div(loop, NL), NX)
    y = lax.div(loop, NL * NX)

    def turn(value, step, count):
        return lax.rem(value + (step % count), count)

    h_next = lax.rem(h + jnp.where(l == NL - 1, 1, 0), NH)
    h_prev = lax.rem(h + jnp.where(l == 0, NH - 1, 0), NH)
    sib_dev = (loop, h * 2 + other)
    next_dev = (lax.rem(loop + 1, BANDS), h_next * 2 + core)
    prev_dev = (lax.rem(loop + BANDS - 1, BANDS), h_prev * 2 + core)
    h_dev = {k: (loop, turn(h, k, NH) * 2 + core) for k in range(1, NH)}
    y_dev = {k: ((turn(y, k, NY) * NX + x) * NL + l, rep) for k in range(1, NY)}
    x_dev = {k: ((y * NX + turn(x, k, NX)) * NL + l, rep) for k in range(1, NX)}
    l_dev = {k: ((y * NX + x) * NL + turn(l, k, NL), rep) for k in range(1, NL)}

    started = []

    def copy(src, dst, name, index, device):
        at = PLAN[name] + index
        return pltpu.make_async_remote_copy(
            src_ref=src, dst_ref=dst, send_sem=ssem.at[at], recv_sem=rsem.at[at],
            device_id=device, device_id_type=MESH,
        )

    def send(src, dst, name, index, device):
        one = copy(src, dst, name, index, device)
        one.start()
        started.append(one)

    def arrived(landing, name, index, device):
        copy(landing, landing, name, index, device).wait_recv()

    feat_in = pltpu.make_async_copy(feat_hbm, feat_ref, local_sem.at[0])
    others_in = [
        pltpu.make_async_copy(src, dst, local_sem.at[1 + at])
        for at, (src, dst) in enumerate(((ws_hbm, ws_ref), (wk_hbm, wk_ref), (cot_hbm, cot_ref)))
    ]
    tiles_in = [
        pltpu.make_async_copy(tiles_hbm.at[0, pl.ds(q * 32, 32)], tiles.at[pl.ds(q * 32, 32)], local_sem.at[4 + q])
        for q in range(4)
    ]
    for one in [feat_in] + tiles_in + others_in:
        one.start()

    barrier = pltpu.get_barrier_semaphore()
    partners = [sib_dev, next_dev, prev_dev]
    for group in (h_dev, y_dev, x_dev, l_dev):
        partners.extend(group.values())
    for device in partners:
        pl.semaphore_signal(barrier, inc=1, device_id=device, device_id_type=MESH)

    slot = lax.broadcasted_iota(jnp.int32, (1, SLOTS), 1)
    row = jnp.zeros((1, SLOTS), jnp.int32)
    for k in range(1, REPS):
        row = row + jnp.where(starts_ref[0, k] <= slot, 1, 0)
    key = row * 32 + (columns_ref[...] - (loop - 1) * REPS)
    key = jnp.where(slot < starts_ref[0, REPS], key, -1)
    key = jnp.broadcast_to(key, (SLOTS, SLOTS)).T
    place = lax.broadcasted_iota(jnp.int32, (SLOTS, SLOTS), 1)
    slot = lax.broadcasted_iota(jnp.int32, (SLOTS, SLOTS), 0) - SLOTS
    for q in range(2):
        found = jnp.sum(jnp.where(key == place + 128 * q, slot, 0), axis=0, keepdims=True)
        table_v[q:q + 1, :] = found + SLOTS
    table_in = pltpu.make_async_copy(table_v, table, local_sem.at[8])
    table_in.start()
    feat_in.wait()
    pl.semaphore_wait(barrier, len(partners))

    mine = f_buf.at[1, h, core]
    for k in (2, 1, 3):
        send(feat_ref, mine, "a_h", k, h_dev[k])
    send(feat_ref, f_buf.at[0, h, core], "a_next", 0, next_dev)
    send(feat_ref, f_buf.at[2, h, core], "a_prev", 0, prev_dev)
    send(feat_ref, mine, "a_sib", 0, sib_dev)
    f_buf[1, h, core] = feat_ref[...]

    tiles[SLOTS] = jnp.zeros((TILE, TILE), BF16)
    table_in.wait()
    for one in tiles_in:
        one.wait()

    def assemble(b, carry):
        rows = pl.ds(pl.multiple_of(b * TILE, TILE), TILE)
        line, first = lax.div(b, 4), lax.rem(b, 4) * 32
        for c in range(SPAN * REPS):
            at = jnp.clip(table[line, first + c], 0, SLOTS)
            a_mat[c // 2, rows, (c % 2) * TILE:(c % 2 + 1) * TILE] = tiles[at]
        return carry

    lax.fori_loop(0, REPS, assemble, 0)
    for one in others_in:
        one.wait()

    def own_block(k):
        return f_buf.at[1, turn(h, -k, NH), core]

    def own_in(k):
        here = own_block(k)
        behind = turn(h, -k, NH)
        arrived(here, "a_h", k, h_dev[k])
        send(here, f_buf.at[0, behind, core], "a_next", k, next_dev)
        send(here, f_buf.at[2, behind, core], "a_prev", k, prev_dev)
        send(here, here, "a_sib", k, sib_dev)

    def beside_in(k):
        before = f_buf.at[0, turn(h_prev, -k, NH), core]
        arrived(before, "a_next", k, prev_dev)
        send(before, before, "a_sib_prev", k, sib_dev)
        after = f_buf.at[2, turn(h_next, -k, NH), core]
        arrived(after, "a_prev", k, next_dev)
        send(after, after, "a_sib_next", k, sib_dev)

    def product(j, at, m):
        rows = pl.ds(pl.multiple_of(m * 256, 256), 256)
        return dot(a_mat[4 * j + at, rows, :], f_buf[j, at].reshape(256, FEAT)).reshape(2, TILE, FEAT)

    def add_own(k, first=False):
        at = turn(h, -k, NH)
        arrived(f_buf.at[1, at, other], "a_sib", k, sib_dev)

        def step(m, carry):
            part = product(1, at, m)
            p_acc[m] = part if first else p_acc[m] + part
            return carry

        lax.fori_loop(0, NH, step, 0)

    def beside_at(k):
        before, after = turn(h_prev, -k, NH), turn(h_next, -k, NH)
        arrived(f_buf.at[0, before, other], "a_sib_prev", k, sib_dev)
        arrived(f_buf.at[2, after, other], "a_sib_next", k, sib_dev)
        return before, after

    def add_beside(k):
        before, after = beside_at(k)

        def step(m, carry):
            p_acc[m] = p_acc[m] + (product(0, before, m) + product(2, after, m))
            return carry

        lax.fori_loop(0, NH, step, 0)

    own_in(1)
    own_in(3)
    beside_in(0)
    add_own(0, first=True)
    own_in(2)
    add_own(1)
    add_own(3)
    beside_in(1)
    beside_in(3)
    add_beside(0)
    add_own(2)
    add_beside(1)
    self_part = dot(feat_ref[...], ws_ref[...])
    beside_in(2)
    add_beside(3)

    before, after = beside_at(2)
    for k in (2, 1, 3, 0):
        m = turn(h, k, NH)
        p_acc[m] = p_acc[m] + (product(0, before, m) + product(2, after, m))
        c_send[k] = p_acc[m, other].astype(BF16)
        send(c_send.at[k], c_sib.at[k], "c_sib", k, sib_dev)
    for k in (2, 1, 3):
        arrived(c_sib.at[k], "c_sib", k, sib_dev)
        c_chip[k] = (p_acc[turn(h, k, NH), core] + c_sib[k].astype(F32)).astype(BF16)
        send(c_chip.at[k], c_recv.at[k], "c_h", k, h_dev[k])
    arrived(c_sib.at[0], "c_sib", 0, sib_dev)
    kernel_sum = p_acc[h, core] + c_sib[0].astype(F32)
    for k in (1, 3, 2):
        arrived(c_recv.at[k], "c_h", k, h_dev[k])
        kernel_sum = kernel_sum + c_recv[k].astype(F32)
    kernel_rows = kernel_sum.astype(BF16)

    preact = self_part + dot(kernel_rows, wk_ref[...])
    root = math.sqrt(2.0 / math.pi)
    square = preact * preact
    bend = jnp.tanh(root * (preact + 0.044715 * (square * preact)))
    half = 0.5 * (1.0 + bend)
    slope = half + 0.5 * preact * (1.0 - bend * bend) * (root * (1.0 + 3.0 * 0.044715 * square))
    grad_pre = (cot_ref[...].astype(F32) * slope).astype(BF16)

    g_t[h, core] = dot_nt(wk_ref[...], grad_pre).astype(BF16)
    mine = g_t.at[h, core]
    for k in (2, 1, 3):
        send(mine, mine, "e_h", k, h_dev[k])
    send(mine, mine, "e_sib", 0, sib_dev)
    out_ref[...] = (preact * half).astype(BF16)

    w_f32[0] = dot_tn(feat_ref[...], grad_pre)
    w_f32[1] = dot_tn(kernel_rows, grad_pre)
    w_send[...] = w_f32[other].astype(BF16)
    send(w_send, w_sib, "w_sib", 0, sib_dev)
    returned = dot_nt(ws_ref[...], grad_pre)

    def gradients(at):
        return jnp.concatenate([g_t[at, 0], g_t[at, 1]], axis=1)

    def back(at, left, n):
        rows = pl.ds(pl.multiple_of(at * 256, 256), 256)
        return dot(left, a_mat[n, rows, :])

    def add_back(k, first=False):
        at = turn(h, -k, NH)
        arrived(g_t.at[at, other], "e_sib", k, sib_dev)
        left = gradients(at)

        def step(n, carry):
            part = back(at, left, n)
            r_acc[n] = part if first else r_acc[n] + part
            return carry

        lax.fori_loop(0, SPAN * NH, step, 0)

    def gradient_in(k):
        here = g_t.at[turn(h, -k, NH), core]
        arrived(here, "e_h", k, h_dev[k])
        send(here, here, "e_sib", k, sib_dev)

    def chip_rows(block):
        rows = pl.ds(pl.multiple_of(block * 32, 32), 32)
        return w_f32[core, rows, :] + w_sib[rows, :].astype(F32)

    arrived(w_sib, "w_sib", 0, sib_dev)
    for k in range(1, NY):
        wy_send[k] = chip_rows(turn(y, k, NY)).astype(BF16)
        send(wy_send.at[k], wy_recv.at[k], "w_y", k, y_dev[k])
    add_back(0, first=True)
    gradient_in(1)
    gradient_in(3)
    add_back(1)
    gradient_in(2)
    for k in range(1, NY):
        arrived(wy_recv.at[k], "w_y", k, y_dev[k])
    part = chip_rows(y)
    for k in range(1, NY):
        part = part + wy_recv[k].astype(F32)
    for q in range(NX):
        wx_send[q] = part[(q // 2) * 16:(q // 2 + 1) * 16, (q % 2) * 128:(q % 2 + 1) * 128]
    for k in range(1, NX):
        send(wx_send.at[turn(x, k, NX)], wx_recv.at[k], "w_x", k, x_dev[k])

    add_back(3)

    for k in range(1, NX):
        arrived(wx_recv.at[k], "w_x", k, x_dev[k])
    part = wx_send[x]
    for k in range(1, NX):
        part = part + wx_recv[k]
    wh_all[h] = part
    for k in (2, 1, 3):
        send(wh_all.at[h], wh_all.at[h], "w_h", k, h_dev[k])

    at = turn(h, -2, NH)
    arrived(g_t.at[at, other], "e_sib", 2, sib_dev)
    left = gradients(at)
    first_core = core == 0

    def backward_band(j):
        for q in range(NH):
            part = r_acc[4 * j + q] + back(at, left, 4 * j + q)
            low, high = part[:, :TILE], part[:, TILE:]
            r_send[j, q] = jnp.where(first_core, high, low).astype(BF16)
            send(r_send.at[j, q], r_sib.at[j, q], "g_sib", 4 * j + q, sib_dev)
            r_own[j, q] = jnp.where(first_core, low, high)

    def to_beside(j, device):
        for q in range(NH):
            arrived(r_sib.at[j, q], "g_sib", 4 * j + q, sib_dev)
            r_chip[j // 2, q] = (r_own[j, q] + r_sib[j, q].astype(F32)).astype(BF16)
            send(r_chip.at[j // 2, q], r_l.at[j // 2, q], "g_l", 2 * j + q, device)

    backward_band(0)
    backward_band(2)
    to_beside(0, prev_dev)
    to_beside(2, next_dev)

    backward_band(1)

    for k in range(1, NH):
        arrived(wh_all.at[turn(h, -k, NH)], "w_h", k, h_dev[k])
    wl_all[l] = (wh_all[0] + wh_all[1]) + (wh_all[2] + wh_all[3])
    for k in range(1, NL):
        send(wl_all.at[l], wl_all.at[l], "w_l", k, l_dev[k])

    for q in range(NH):
        arrived(r_sib.at[1, q], "g_sib", 4 + q, sib_dev)
    r_own[1] = r_own[1] + r_sib[1].astype(F32)

    for k in range(1, NL):
        arrived(wl_all.at[turn(l, -k, NL)], "w_l", k, l_dev[k])
    vx_all[x] = (wl_all[0] + wl_all[1] + wl_all[2]).astype(BF16)
    for k in range(1, NX):
        send(vx_all.at[x], vx_all.at[x], "v_x", k, x_dev[k])
    for q in range(NH):
        arrived(r_l.at[0, q], "g_l", q, next_dev)
        arrived(r_l.at[1, q], "g_l", 4 + q, prev_dev)

    def summed(block):
        return r_own[1, block] + (r_l[0, block].astype(F32) + r_l[1, block].astype(F32))

    for k in (2, 1, 3):
        r_hs[k] = summed(turn(h, k, NH)).astype(BF16)
        send(r_hs.at[k], r_h.at[k], "g_h", k, h_dev[k])
    returned = returned + summed(h)

    for k in range(1, NX):
        arrived(vx_all.at[turn(x, -k, NX)], "v_x", k, x_dev[k])
    vy_all[y] = jnp.concatenate(
        [jnp.concatenate([vx_all[2 * q], vx_all[2 * q + 1]], axis=1) for q in range(NX // 2)], axis=0
    )
    for k in range(1, NY):
        send(vy_all.at[y], vy_all.at[y], "v_y", k, y_dev[k])

    for k in (1, 3, 2):
        arrived(r_h.at[k], "g_h", k, h_dev[k])
        returned = returned + r_h[k].astype(F32)
    fg_ref[...] = returned.T.astype(BF16)

    for k in range(1, NY):
        arrived(vy_all.at[turn(y, -k, NY)], "v_y", k, y_dev[k])
    v_mat[core] = vy_all[...].reshape(FEAT, FEAT)
    send(v_mat.at[core], v_mat.at[core], "v_sib", 0, sib_dev)
    scale = 1.0 / math.sqrt(TILE * REPS * BANDS)
    wg_ref[core] = v_mat[core].astype(F32) * scale
    arrived(v_mat.at[other], "v_sib", 0, sib_dev)
    wg_ref[other] = v_mat[other].astype(F32) * scale

    for one in started:
        one.wait_send()


def scratch():
    return [
        pltpu.VMEM((TILE, FEAT), BF16),
        pltpu.VMEM((FEAT, FEAT), BF16),
        pltpu.VMEM((FEAT, FEAT), BF16),
        pltpu.VMEM((TILE, FEAT), BF16),
        pltpu.VMEM((2, 128), jnp.int32),
        pltpu.SMEM((2, 128), jnp.int32),
        pltpu.VMEM((SLOTS + 1, TILE, TILE), BF16),
        pltpu.VMEM((SPAN * NH, REPS * TILE, 2 * TILE), BF16),
        pltpu.VMEM((SPAN, NH, 2, TILE, FEAT), BF16),
        pltpu.VMEM((NH, 2, TILE, FEAT), F32),
        pltpu.VMEM((NH, TILE, FEAT), BF16),
        pltpu.VMEM((NH, TILE, FEAT), BF16),
        pltpu.VMEM((NH, TILE, FEAT), BF16),
        pltpu.VMEM((NH, TILE, FEAT), BF16),
        pltpu.VMEM((NH, 2, FEAT, TILE), BF16),
        pltpu.VMEM((SPAN * NH, FEAT, 2 * TILE), F32),
        pltpu.VMEM((SPAN, NH, FEAT, TILE), F32),
        pltpu.VMEM((SPAN, NH, FEAT, TILE), BF16),
        pltpu.VMEM((SPAN, NH, FEAT, TILE), BF16),
        pltpu.VMEM((2, NH, FEAT, TILE), BF16),
        pltpu.VMEM((2, NH, FEAT, TILE), BF16),
        pltpu.VMEM((NH, FEAT, TILE), BF16),
        pltpu.VMEM((NH, FEAT, TILE), BF16),
        pltpu.VMEM((2, FEAT, FEAT), F32),
        pltpu.VMEM((FEAT, FEAT), BF16),
        pltpu.VMEM((FEAT, FEAT), BF16),
        pltpu.VMEM((NY, 32, FEAT), BF16),
        pltpu.VMEM((NY, 32, FEAT), BF16),
        pltpu.VMEM((NX, 16, 128), F32),
        pltpu.VMEM((NX, 16, 128), F32),
        pltpu.VMEM((NH, 16, 128), F32),
        pltpu.VMEM((NL, 16, 128), F32),
        pltpu.VMEM((NX, 16, 128), BF16),
        pltpu.VMEM((NY, 32, FEAT), BF16),
        pltpu.VMEM((2, FEAT, FEAT), BF16),
        pltpu.SemaphoreType.DMA((9,)),
        pltpu.SemaphoreType.DMA((N_SEMS,)),
        pltpu.SemaphoreType.DMA((N_SEMS,)),
    ]


def hand_out(*refs):
    results, outputs, held, sem = refs[:3], refs[3:6], refs[6:9], refs[9]
    ins = [pltpu.make_async_copy(results[at], held[at], sem.at[at]) for at in range(3)]
    outs = [pltpu.make_async_copy(held[at], outputs[at], sem.at[3 + at]) for at in range(3)]
    for one in ins:
        one.start()
    for at in range(3):
        ins[at].wait()
        outs[at].start()
    for one in outs:
        one.wait()


def on_device(features, kernel_tiles, row_starts, column_block, self_weight, kernel_weight, cotangent):
    vmem = pl.BlockSpec(memory_space=pltpu.VMEM)
    hbm = pl.BlockSpec(memory_space=pltpu.HBM)
    shapes = (
        jax.ShapeDtypeStruct((TILE, FEAT), BF16),
        jax.ShapeDtypeStruct((TILE, FEAT), BF16),
        jax.ShapeDtypeStruct((2, FEAT, FEAT), F32),
    )
    results = pl.pallas_call(
        kernel,
        out_shape=shapes,
        in_specs=[pl.BlockSpec(memory_space=pltpu.SMEM), vmem, hbm, hbm, hbm, hbm, hbm],
        out_specs=(vmem, vmem, vmem),
        scratch_shapes=scratch(),
        compiler_params=pltpu.CompilerParams(
            collective_id=0, has_side_effects=True, vmem_limit_bytes=64 * 1024 * 1024 - 65536
        ),
    )(row_starts, column_block, features, self_weight, kernel_weight, cotangent, kernel_tiles)
    return pl.pallas_call(
        hand_out,
        out_shape=shapes,
        in_specs=[pl.BlockSpec(memory_space=pl.ANY)] * 3,
        out_specs=(pl.BlockSpec(memory_space=pl.ANY),) * 3,
        scratch_shapes=[pltpu.VMEM(one.shape, one.dtype) for one in shapes] + [pltpu.SemaphoreType.DMA((6,))],
        compiler_params=pltpu.CompilerParams(vmem_limit_bytes=64 * 1024 * 1024 - 65536),
    )(*results)


def solution(mesh):
    split = P(("loop", "rep"), None)
    return jax.shard_map(
        on_device,
        mesh=mesh,
        in_specs=(split, P(("loop", "rep"), None, None, None), split, split, P(), P(), split),
        out_specs=(split, split, P()),
        check_vma=False,
    )
```

```python
import math

import jax
import jax.numpy as jnp
from jax import lax
from jax.experimental import pallas as pl
from jax.experimental.pallas import tpu as pltpu
from jax.sharding import PartitionSpec as P

MESH = pl.DeviceIdType.MESH
BF16 = jnp.bfloat16
F32 = jnp.float32

NL, NX, NY, NH = 3, 4, 8, 4
BANDS = NL * NX * NY
REPS = NH * 2
TILE = 128
FEAT = 256
SLOTS = 128
SPAN = 3
ROWS = REPS * TILE


def sem_plan():
    plan, count = {}, 0
    for name, number in (
        ("a_h", 4), ("a_sib", 4), ("a_next", 4), ("a_prev", 4), ("a_sib_prev", 4), ("a_sib_next", 4),
        ("c_sib", 4), ("c_h", 4), ("e_h", 4), ("e_sib", 4),
        ("g_sib", 12), ("g_l", 8), ("g_h", 4),
        ("w_sib", 1), ("w_y", 8), ("w_x", 4), ("w_h", 4), ("w_l", 3),
        ("v_y", 8), ("v_sib", 1),
    ):
        plan[name] = count
        count += number
    return plan, count


PLAN, N_SEMS = sem_plan()


def dot(a, b):
    return jnp.dot(a, b, preferred_element_type=F32)


def dot_nt(a, b):
    return lax.dot_general(a, b, (((1,), (1,)), ((), ())), preferred_element_type=F32)


def dot_tn(a, b):
    return lax.dot_general(a, b, (((0,), (0,)), ((), ())), preferred_element_type=F32)


def kernel(
    starts_ref, columns_ref, feat_hbm, ws_hbm, wk_hbm, cot_hbm, tiles_hbm,
    out_hbm, fg_hbm, wg_hbm,
    out_ref, fg_ref, wg_ref, feat_ref, ws_ref, wk_ref, cot_ref, table_v, table,
    tiles, a_mat, f_buf, p_acc, c_send, c_sib, c_chip, c_recv,
    g_t, r_acc, r_own, r_send, r_sib, r_chip, r_l, r_hs, r_h,
    w_f32, w_send, w_sib, wy_send, wy_recv, wx_all, wh_all, wl_all, vy_all, v_mat,
    local_sem, ssem, rsem,
):
    loop = lax.axis_index("loop")
    rep = lax.axis_index("rep")
    core = lax.rem(rep, 2)
    other = 1 - core
    h = lax.div(rep, 2)
    l = lax.rem(loop, NL)
    x = lax.rem(lax.div(loop, NL), NX)
    y = lax.div(loop, NL * NX)

    def turn(value, step, count):
        return lax.rem(value + (step % count), count)

    h_next = lax.rem(h + jnp.where(l == NL - 1, 1, 0), NH)
    h_prev = lax.rem(h + jnp.where(l == 0, NH - 1, 0), NH)
    sib_dev = (loop, h * 2 + other)
    next_dev = (lax.rem(loop + 1, BANDS), h_next * 2 + core)
    prev_dev = (lax.rem(loop + BANDS - 1, BANDS), h_prev * 2 + core)
    h_dev = {k: (loop, turn(h, k, NH) * 2 + core) for k in range(1, NH)}
    y_dev = {k: ((turn(y, k, NY) * NX + x) * NL + l, rep) for k in range(1, NY)}
    x_dev = {k: ((y * NX + turn(x, k, NX)) * NL + l, rep) for k in range(1, NX)}
    l_dev = {k: ((y * NX + x) * NL + turn(l, k, NL), rep) for k in range(1, NL)}

    started = []

    def copy(src, dst, name, index, device):
        at = PLAN[name] + index
        return pltpu.make_async_remote_copy(
            src_ref=src, dst_ref=dst, send_sem=ssem.at[at], recv_sem=rsem.at[at],
            device_id=device, device_id_type=MESH,
        )

    def send(src, dst, name, index, device):
        one = copy(src, dst, name, index, device)
        one.start()
        started.append(one)

    def arrived(landing, name, index, device):
        copy(landing, landing, name, index, device).wait_recv()

    given = []

    def give(src, dst, index):
        one = pltpu.make_async_copy(src, dst, local_sem.at[9 + index])
        one.start()
        given.append(one)

    feat_in = pltpu.make_async_copy(feat_hbm, feat_ref, local_sem.at[0])
    others_in = [
        pltpu.make_async_copy(src, dst, local_sem.at[1 + at])
        for at, (src, dst) in enumerate(((ws_hbm, ws_ref), (wk_hbm, wk_ref), (cot_hbm, cot_ref)))
    ]
    tiles_in = [
        pltpu.make_async_copy(tiles_hbm.at[0, pl.ds(q * 32, 32)], tiles.at[pl.ds(q * 32, 32)], local_sem.at[4 + q])
        for q in range(4)
    ]
    for one in [feat_in] + tiles_in + others_in:
        one.start()

    barrier = pltpu.get_barrier_semaphore()
    partners = [sib_dev, next_dev, prev_dev]
    for group in (h_dev, y_dev, x_dev, l_dev):
        partners.extend(group.values())
    for device in partners:
        pl.semaphore_signal(barrier, inc=1, device_id=device, device_id_type=MESH)

    slot = lax.broadcasted_iota(jnp.int32, (1, SLOTS), 1)
    row = jnp.zeros((1, SLOTS), jnp.int32)
    for k in range(1, REPS):
        row = row + jnp.where(starts_ref[0, k] <= slot, 1, 0)
    key = row * 32 + (columns_ref[...] - (loop - 1) * REPS)
    key = jnp.where(slot < starts_ref[0, REPS], key, -1)
    key = jnp.broadcast_to(key, (SLOTS, SLOTS)).T
    place = lax.broadcasted_iota(jnp.int32, (SLOTS, SLOTS), 1)
    slot = lax.broadcasted_iota(jnp.int32, (SLOTS, SLOTS), 0) - SLOTS
    for q in range(2):
        found = jnp.sum(jnp.where(key == place + 128 * q, slot, 0), axis=0, keepdims=True)
        table_v[q:q + 1, :] = found + SLOTS
    table_in = pltpu.make_async_copy(table_v, table, local_sem.at[8])
    table_in.start()
    feat_in.wait()
    pl.semaphore_wait(barrier, len(partners))

    mine = f_buf.at[1, h, core]
    for k in (2, 1, 3):
        send(feat_ref, mine, "a_h", k, h_dev[k])
    send(feat_ref, f_buf.at[0, h, core], "a_next", 0, next_dev)
    send(feat_ref, f_buf.at[2, h, core], "a_prev", 0, prev_dev)
    send(feat_ref, mine, "a_sib", 0, sib_dev)
    f_buf[1, h, core] = feat_ref[...]

    tiles[SLOTS] = jnp.zeros((TILE, TILE), BF16)
    table_in.wait()
    for one in tiles_in:
        one.wait()

    def assemble(b, carry):
        rows = pl.ds(pl.multiple_of(b * TILE, TILE), TILE)
        line, first = lax.div(b, 4), lax.rem(b, 4) * 32
        for c in range(SPAN * REPS):
            at = jnp.clip(table[line, first + c], 0, SLOTS)
            a_mat[c // 2, rows, (c % 2) * TILE:(c % 2 + 1) * TILE] = tiles[at]
        return carry

    lax.fori_loop(0, REPS, assemble, 0)
    for one in others_in:
        one.wait()

    def own_block(k):
        return f_buf.at[1, turn(h, -k, NH), core]

    def own_in(k):
        here = own_block(k)
        behind = turn(h, -k, NH)
        arrived(here, "a_h", k, h_dev[k])
        send(here, f_buf.at[0, behind, core], "a_next", k, next_dev)
        send(here, f_buf.at[2, behind, core], "a_prev", k, prev_dev)
        send(here, here, "a_sib", k, sib_dev)

    def beside_in(k):
        before = f_buf.at[0, turn(h_prev, -k, NH), core]
        arrived(before, "a_next", k, prev_dev)
        send(before, before, "a_sib_prev", k, sib_dev)
        after = f_buf.at[2, turn(h_next, -k, NH), core]
        arrived(after, "a_prev", k, next_dev)
        send(after, after, "a_sib_next", k, sib_dev)

    def product(j, at, m):
        rows = pl.ds(pl.multiple_of(m * 256, 256), 256)
        return dot(a_mat[4 * j + at, rows, :], f_buf[j, at].reshape(256, FEAT)).reshape(2, TILE, FEAT)

    def add_own(*turns):
        places = [turn(h, -k, NH) for k in turns]
        for k, at in zip(turns, places):
            arrived(f_buf.at[1, at, other], "a_sib", k, sib_dev)

        def step(m, carry):
            part = product(1, places[0], m)
            for at in places[1:]:
                part = part + product(1, at, m)
            p_acc[m] = part if turns == (0,) else p_acc[m] + part
            return carry

        lax.fori_loop(0, NH, step, 0, unroll=True)

    def beside_at(k):
        before, after = turn(h_prev, -k, NH), turn(h_next, -k, NH)
        arrived(f_buf.at[0, before, other], "a_sib_prev", k, sib_dev)
        arrived(f_buf.at[2, after, other], "a_sib_next", k, sib_dev)
        return before, after

    def add_beside(k):
        before, after = beside_at(k)

        def step(m, carry):
            p_acc[m] = p_acc[m] + (product(0, before, m) + product(2, after, m))
            return carry

        lax.fori_loop(0, NH, step, 0, unroll=True)

    own_in(1)
    own_in(3)
    beside_in(0)
    add_own(0)
    own_in(2)
    add_own(1, 3)
    beside_in(1)
    beside_in(3)
    add_beside(0)
    add_own(2)
    add_beside(1)
    self_part = dot(feat_ref[...], ws_ref[...])
    beside_in(2)
    add_beside(3)

    before, after = beside_at(2)
    for k in (2, 1, 3, 0):
        m = turn(h, k, NH)
        p_acc[m] = p_acc[m] + (product(0, before, m) + product(2, after, m))
        c_send[k] = p_acc[m, other].astype(BF16)
        send(c_send.at[k], c_sib.at[k], "c_sib", k, sib_dev)
    for k in (2, 1, 3):
        arrived(c_sib.at[k], "c_sib", k, sib_dev)
        c_chip[k] = (p_acc[turn(h, k, NH), core] + c_sib[k].astype(F32)).astype(BF16)
        send(c_chip.at[k], c_recv.at[k], "c_h", k, h_dev[k])
    arrived(c_sib.at[0], "c_sib", 0, sib_dev)
    kernel_sum = p_acc[h, core] + c_sib[0].astype(F32)
    for k in (1, 3, 2):
        arrived(c_recv.at[k], "c_h", k, h_dev[k])
        kernel_sum = kernel_sum + c_recv[k].astype(F32)
    kernel_rows = kernel_sum.astype(BF16)

    preact = self_part + dot(kernel_rows, wk_ref[...])
    root = math.sqrt(2.0 / math.pi)
    square = preact * preact
    bend = jnp.tanh(root * (preact + 0.044715 * (square * preact)))
    half = 0.5 * (1.0 + bend)
    slope = half + 0.5 * preact * (1.0 - bend * bend) * (root * (1.0 + 3.0 * 0.044715 * square))
    grad_pre = (cot_ref[...].astype(F32) * slope).astype(BF16)

    g_t[h, core] = dot_nt(wk_ref[...], grad_pre).astype(BF16)
    mine = g_t.at[h, core]
    for k in (2, 1, 3):
        send(mine, mine, "e_h", k, h_dev[k])
    send(mine, mine, "e_sib", 0, sib_dev)
    out_ref[...] = (preact * half).astype(BF16)
    give(out_ref, out_hbm, 0)

    w_f32[0] = dot_tn(feat_ref[...], grad_pre)
    w_f32[1] = dot_tn(kernel_rows, grad_pre)
    w_send[...] = w_f32[other].astype(BF16)
    send(w_send, w_sib, "w_sib", 0, sib_dev)
    returned = dot_nt(ws_ref[...], grad_pre)

    def gradients(at):
        return jnp.concatenate([g_t[at, 0], g_t[at, 1]], axis=1)

    def back(at, left, n):
        rows = pl.ds(pl.multiple_of(at * 256, 256), 256)
        return dot(left, a_mat[n, rows, :])

    def add_back(*turns):
        places = [turn(h, -k, NH) for k in turns]
        for k, at in zip(turns, places):
            arrived(g_t.at[at, other], "e_sib", k, sib_dev)
        lefts = [gradients(at) for at in places]

        def step(n, carry):
            part = back(places[0], lefts[0], n)
            for at, left in zip(places[1:], lefts[1:]):
                part = part + back(at, left, n)
            r_acc[n] = part if turns == (0,) else r_acc[n] + part
            return carry

        lax.fori_loop(0, SPAN * NH, step, 0, unroll=True)

    def gradient_in(k):
        here = g_t.at[turn(h, -k, NH), core]
        arrived(here, "e_h", k, h_dev[k])
        send(here, here, "e_sib", k, sib_dev)

    def total(parts, count):
        one = parts[0].astype(F32)
        for q in range(1, count):
            one = one + parts[q].astype(F32)
        return one.astype(BF16)

    def chip_rows(block):
        rows = pl.ds(pl.multiple_of(block * 32, 32), 32)
        return w_f32[core, rows, :] + w_sib[rows, :].astype(F32)

    arrived(w_sib, "w_sib", 0, sib_dev)
    for k in range(1, NY):
        wy_send[k] = chip_rows(turn(y, k, NY)).astype(BF16)
        send(wy_send.at[k], wy_recv.at[k], "w_y", k, y_dev[k])
    add_back(0)
    gradient_in(1)
    gradient_in(3)
    add_back(1)
    gradient_in(2)

    for k in range(1, NY):
        arrived(wy_recv.at[k], "w_y", k, y_dev[k])
    part = chip_rows(y)
    for k in range(1, NY):
        part = part + wy_recv[k].astype(F32)
    wx_all[x] = part.astype(BF16)
    for k in range(1, NX):
        send(wx_all.at[x], wx_all.at[x], "w_x", k, x_dev[k])

    add_back(3)

    at = turn(h, -2, NH)
    arrived(g_t.at[at, other], "e_sib", 2, sib_dev)
    left = gradients(at)
    first_core = core == 0

    def products_back(j, base, k):
        q = turn(base, k, NH)
        part = r_acc[4 * j + q] + back(at, left, 4 * j + q)
        low, high = part[:, :TILE], part[:, TILE:]
        r_send[j, k] = jnp.where(first_core, high, low).astype(BF16)
        send(r_send.at[j, k], r_sib.at[j, k], "g_sib", 4 * j + k, sib_dev)
        r_own[j, k] = jnp.where(first_core, low, high)

    def to_beside(j, k, device):
        arrived(r_sib.at[j, k], "g_sib", 4 * j + k, sib_dev)
        r_chip[j // 2, k] = (r_own[j, k] + r_sib[j, k].astype(F32)).astype(BF16)
        send(r_chip.at[j // 2, k], r_l.at[j // 2, k], "g_l", 2 * j + k, device)

    def summed(k):
        arrived(r_sib.at[1, k], "g_sib", 4 + k, sib_dev)
        arrived(r_l.at[0, k], "g_l", k, next_dev)
        arrived(r_l.at[1, k], "g_l", 4 + k, prev_dev)
        return (r_own[1, k] + r_sib[1, k].astype(F32)) + (r_l[0, k].astype(F32) + r_l[1, k].astype(F32))

    def to_holder(k):
        r_hs[k] = summed(k).astype(BF16)
        send(r_hs.at[k], r_h.at[k], "g_h", k, h_dev[k])

    order = (2, 1, 3, 0)
    for step, k in enumerate(order):
        products_back(0, h_prev, k)
        products_back(2, h_next, k)
        if step > 0:
            to_beside(0, order[step - 1], prev_dev)
            to_beside(2, order[step - 1], next_dev)
        if step == 1:
            for q in range(1, NX):
                arrived(wx_all.at[turn(x, -q, NX)], "w_x", q, x_dev[q])
            wh_all[h] = total(wx_all, NX)
            for q in (2, 1, 3):
                send(wh_all.at[h], wh_all.at[h], "w_h", q, h_dev[q])
    products_back(1, h, 2)
    to_beside(0, 0, prev_dev)
    to_beside(2, 0, next_dev)
    for k in (1, 3, 0):
        products_back(1, h, k)

    for k in range(1, NH):
        arrived(wh_all.at[turn(h, -k, NH)], "w_h", k, h_dev[k])
    wl_all[l] = total(wh_all, NH)
    for k in range(1, NL):
        send(wl_all.at[l], wl_all.at[l], "w_l", k, l_dev[k])

    to_holder(2)

    for k in range(1, NL):
        arrived(wl_all.at[turn(l, -k, NL)], "w_l", k, l_dev[k])
    vy_all[y] = total(wl_all, NL)
    for k in range(1, NY):
        send(vy_all.at[y], vy_all.at[y], "v_y", k, y_dev[k])

    to_holder(1)
    to_holder(3)
    returned = returned + summed(0)

    settled = len(started) - 2 * NY
    for one in started[:settled]:
        one.wait_send()

    for k in (1, 3, 2):
        arrived(r_h.at[k], "g_h", k, h_dev[k])
        returned = returned + r_h[k].astype(F32)
    fg_ref[...] = returned.T.astype(BF16)
    give(fg_ref, fg_hbm, 1)

    for k in range(1, NY):
        arrived(vy_all.at[turn(y, -k, NY)], "v_y", k, y_dev[k])
    v_mat[core] = vy_all[...].reshape(FEAT, FEAT)
    send(v_mat.at[core], v_mat.at[core], "v_sib", 0, sib_dev)
    scale = 1.0 / math.sqrt(TILE * REPS * BANDS)
    wg_ref[core] = v_mat[core].astype(F32) * scale
    give(wg_ref.at[core], wg_hbm.at[core], 2)
    arrived(v_mat.at[other], "v_sib", 0, sib_dev)
    wg_ref[other] = v_mat[other].astype(F32) * scale
    give(wg_ref.at[other], wg_hbm.at[other], 3)

    for one in started[settled:]:
        one.wait_send()
    for one in given:
        one.wait()


def scratch():
    return [
        pltpu.VMEM((TILE, FEAT), BF16),
        pltpu.VMEM((TILE, FEAT), BF16),
        pltpu.VMEM((2, FEAT, FEAT), F32),
        pltpu.VMEM((TILE, FEAT), BF16),
        pltpu.VMEM((FEAT, FEAT), BF16),
        pltpu.VMEM((FEAT, FEAT), BF16),
        pltpu.VMEM((TILE, FEAT), BF16),
        pltpu.VMEM((2, 128), jnp.int32),
        pltpu.SMEM((2, 128), jnp.int32),
        pltpu.VMEM((SLOTS + 1, TILE, TILE), BF16),
        pltpu.VMEM((SPAN * NH, REPS * TILE, 2 * TILE), BF16),
        pltpu.VMEM((SPAN, NH, 2, TILE, FEAT), BF16),
        pltpu.VMEM((NH, 2, TILE, FEAT), F32),
        pltpu.VMEM((NH, TILE, FEAT), BF16),
        pltpu.VMEM((NH, TILE, FEAT), BF16),
        pltpu.VMEM((NH, TILE, FEAT), BF16),
        pltpu.VMEM((NH, TILE, FEAT), BF16),
        pltpu.VMEM((NH, 2, FEAT, TILE), BF16),
        pltpu.VMEM((SPAN * NH, FEAT, 2 * TILE), F32),
        pltpu.VMEM((SPAN, NH, FEAT, TILE), F32),
        pltpu.VMEM((SPAN, NH, FEAT, TILE), BF16),
        pltpu.VMEM((SPAN, NH, FEAT, TILE), BF16),
        pltpu.VMEM((2, NH, FEAT, TILE), BF16),
        pltpu.VMEM((2, NH, FEAT, TILE), BF16),
        pltpu.VMEM((NH, FEAT, TILE), BF16),
        pltpu.VMEM((NH, FEAT, TILE), BF16),
        pltpu.VMEM((2, FEAT, FEAT), F32),
        pltpu.VMEM((FEAT, FEAT), BF16),
        pltpu.VMEM((FEAT, FEAT), BF16),
        pltpu.VMEM((NY, 32, FEAT), BF16),
        pltpu.VMEM((NY, 32, FEAT), BF16),
        pltpu.VMEM((NX, 32, FEAT), BF16),
        pltpu.VMEM((NH, 32, FEAT), BF16),
        pltpu.VMEM((NL, 32, FEAT), BF16),
        pltpu.VMEM((NY, 32, FEAT), BF16),
        pltpu.VMEM((2, FEAT, FEAT), BF16),
        pltpu.SemaphoreType.DMA((13,)),
        pltpu.SemaphoreType.DMA((N_SEMS,)),
        pltpu.SemaphoreType.DMA((N_SEMS,)),
    ]


def hand_out(*refs):
    results, outputs, held, sem = refs[:3], refs[3:6], refs[6:9], refs[9]
    ins = [pltpu.make_async_copy(results[at], held[at], sem.at[at]) for at in range(3)]
    outs = [pltpu.make_async_copy(held[at], outputs[at], sem.at[3 + at]) for at in range(3)]
    for one in ins:
        one.start()
    for at in range(3):
        ins[at].wait()
        outs[at].start()
    for one in outs:
        one.wait()


def on_device(features, kernel_tiles, row_starts, column_block, self_weight, kernel_weight, cotangent):
    vmem = pl.BlockSpec(memory_space=pltpu.VMEM)
    hbm = pl.BlockSpec(memory_space=pltpu.HBM)
    shapes = (
        jax.ShapeDtypeStruct((TILE, FEAT), BF16),
        jax.ShapeDtypeStruct((TILE, FEAT), BF16),
        jax.ShapeDtypeStruct((2, FEAT, FEAT), F32),
    )
    results = pl.pallas_call(
        kernel,
        out_shape=shapes,
        in_specs=[pl.BlockSpec(memory_space=pltpu.SMEM), vmem, hbm, hbm, hbm, hbm, hbm],
        out_specs=(pl.BlockSpec(memory_space=pl.ANY),) * 3,
        scratch_shapes=scratch(),
        compiler_params=pltpu.CompilerParams(
            collective_id=0, has_side_effects=True, vmem_limit_bytes=64 * 1024 * 1024 - 65536
        ),
    )(row_starts, column_block, features, self_weight, kernel_weight, cotangent, kernel_tiles)
    return pl.pallas_call(
        hand_out,
        out_shape=shapes,
        in_specs=[pl.BlockSpec(memory_space=pl.ANY)] * 3,
        out_specs=(pl.BlockSpec(memory_space=pl.ANY),) * 3,
        scratch_shapes=[pltpu.VMEM(one.shape, one.dtype) for one in shapes] + [pltpu.SemaphoreType.DMA((6,))],
        compiler_params=pltpu.CompilerParams(vmem_limit_bytes=64 * 1024 * 1024 - 65536),
    )(*results)


def solution(mesh):
    split = P(("loop", "rep"), None)
    return jax.shard_map(
        on_device,
        mesh=mesh,
        in_specs=(split, P(("loop", "rep"), None, None, None), split, split, P(), P(), split),
        out_specs=(split, split, P()),
        check_vma=False,
    )
```

```python
import math

import jax
import jax.numpy as jnp
from jax import lax
from jax.experimental import pallas as pl
from jax.experimental.pallas import tpu as pltpu
from jax.sharding import PartitionSpec as P

MESH = pl.DeviceIdType.MESH
BF16 = jnp.bfloat16
F32 = jnp.float32

NL, NX, NY, NH = 3, 4, 8, 4
BANDS = NL * NX * NY
REPS = NH * 2
TILE = 128
FEAT = 256
SLOTS = 128
SPAN = 3
ROWS = REPS * TILE


def sem_plan():
    plan, count = {}, 0
    for name, number in (
        ("a_h", 4), ("a_sib", 4), ("a_next", 4), ("a_prev", 4), ("a_sib_prev", 4), ("a_sib_next", 4),
        ("c_sib", 4), ("c_h", 4), ("e_h", 4), ("e_sib", 4),
        ("g_sib", 12), ("g_l", 8), ("g_h", 4),
        ("w_sib", 1), ("w_y", 8), ("w_x", 4), ("w_h", 4), ("w_l", 3),
        ("v_y", 8), ("v_sib", 1),
    ):
        plan[name] = count
        count += number
    return plan, count


PLAN, N_SEMS = sem_plan()


def dot(a, b):
    return jnp.dot(a, b, preferred_element_type=F32)


def dot_nt(a, b):
    return lax.dot_general(a, b, (((1,), (1,)), ((), ())), preferred_element_type=F32)


def dot_tn(a, b):
    return lax.dot_general(a, b, (((0,), (0,)), ((), ())), preferred_element_type=F32)


def kernel(
    starts_ref, columns_ref, feat_hbm, ws_hbm, wk_hbm, cot_hbm, tiles_hbm,
    out_hbm, fg_hbm, wg_hbm,
    out_ref, fg_ref, wg_ref, feat_ref, ws_ref, wk_ref, cot_ref, table_v, table,
    tiles, a_mat, f_buf, p_acc, c_send, c_sib, c_chip, c_recv,
    g_t, r_acc, r_own, r_send, r_sib, r_chip, r_l, r_hs, r_h,
    w_f32, w_send, w_sib, wy_send, wy_recv, wx_all, wh_all, wl_all, vy_all, v_mat,
    local_sem, ssem, rsem,
):
    loop = lax.axis_index("loop")
    rep = lax.axis_index("rep")
    core = lax.rem(rep, 2)
    other = 1 - core
    h = lax.div(rep, 2)
    l = lax.rem(loop, NL)
    x = lax.rem(lax.div(loop, NL), NX)
    y = lax.div(loop, NL * NX)

    def turn(value, step, count):
        return lax.rem(value + (step % count), count)

    h_next = lax.rem(h + jnp.where(l == NL - 1, 1, 0), NH)
    h_prev = lax.rem(h + jnp.where(l == 0, NH - 1, 0), NH)
    sib_dev = (loop, h * 2 + other)
    next_dev = (lax.rem(loop + 1, BANDS), h_next * 2 + core)
    prev_dev = (lax.rem(loop + BANDS - 1, BANDS), h_prev * 2 + core)
    h_dev = {k: (loop, turn(h, k, NH) * 2 + core) for k in range(1, NH)}
    y_dev = {k: ((turn(y, k, NY) * NX + x) * NL + l, rep) for k in range(1, NY)}
    x_dev = {k: ((y * NX + turn(x, k, NX)) * NL + l, rep) for k in range(1, NX)}
    l_dev = {k: ((y * NX + x) * NL + turn(l, k, NL), rep) for k in range(1, NL)}

    started = []

    def copy(src, dst, name, index, device):
        at = PLAN[name] + index
        return pltpu.make_async_remote_copy(
            src_ref=src, dst_ref=dst, send_sem=ssem.at[at], recv_sem=rsem.at[at],
            device_id=device, device_id_type=MESH,
        )

    def send(src, dst, name, index, device):
        one = copy(src, dst, name, index, device)
        one.start()
        started.append(one)

    def arrived(landing, name, index, device):
        copy(landing, landing, name, index, device).wait_recv()

    given = []

    def give(src, dst, index):
        one = pltpu.make_async_copy(src, dst, local_sem.at[9 + index])
        one.start()
        given.append(one)

    feat_in = pltpu.make_async_copy(feat_hbm, feat_ref, local_sem.at[0])
    others_in = [
        pltpu.make_async_copy(src, dst, local_sem.at[1 + at])
        for at, (src, dst) in enumerate(((ws_hbm, ws_ref), (wk_hbm, wk_ref), (cot_hbm, cot_ref)))
    ]
    tiles_in = [
        pltpu.make_async_copy(tiles_hbm.at[0, pl.ds(q * 32, 32)], tiles.at[pl.ds(q * 32, 32)], local_sem.at[4 + q])
        for q in range(4)
    ]
    for one in [feat_in] + tiles_in + others_in:
        one.start()

    barrier = pltpu.get_barrier_semaphore()
    partners = [sib_dev, next_dev, prev_dev]
    for group in (h_dev, y_dev, x_dev, l_dev):
        partners.extend(group.values())
    for device in partners:
        pl.semaphore_signal(barrier, inc=1, device_id=device, device_id_type=MESH)

    slot = lax.broadcasted_iota(jnp.int32, (1, SLOTS), 1)
    row = jnp.zeros((1, SLOTS), jnp.int32)
    for k in range(1, REPS):
        row = row + jnp.where(starts_ref[0, k] <= slot, 1, 0)
    key = row * 32 + (columns_ref[...] - (loop - 1) * REPS)
    key = jnp.where(slot < starts_ref[0, REPS], key, -1)
    key = jnp.broadcast_to(key, (SLOTS, SLOTS)).T
    place = lax.broadcasted_iota(jnp.int32, (SLOTS, SLOTS), 1)
    slot = lax.broadcasted_iota(jnp.int32, (SLOTS, SLOTS), 0) - SLOTS
    for q in range(2):
        found = jnp.sum(jnp.where(key == place + 128 * q, slot, 0), axis=0, keepdims=True)
        table_v[q:q + 1, :] = found + SLOTS
    table_in = pltpu.make_async_copy(table_v, table, local_sem.at[8])
    table_in.start()
    feat_in.wait()
    pl.semaphore_wait(barrier, len(partners))

    mine = f_buf.at[1, h, core]
    for k in (2, 1, 3):
        send(feat_ref, mine, "a_h", k, h_dev[k])
    send(feat_ref, f_buf.at[0, h, core], "a_next", 0, next_dev)
    send(feat_ref, f_buf.at[2, h, core], "a_prev", 0, prev_dev)
    send(feat_ref, mine, "a_sib", 0, sib_dev)
    f_buf[1, h, core] = feat_ref[...]

    tiles[SLOTS] = jnp.zeros((TILE, TILE), BF16)
    table_in.wait()
    for one in tiles_in:
        one.wait()

    def assemble(b, carry):
        rows = pl.ds(pl.multiple_of(b * TILE, TILE), TILE)
        line, first = lax.div(b, 4), lax.rem(b, 4) * 32
        for c in range(SPAN * REPS):
            at = jnp.clip(table[line, first + c], 0, SLOTS)
            a_mat[c // 2, rows, (c % 2) * TILE:(c % 2 + 1) * TILE] = tiles[at]
        return carry

    lax.fori_loop(0, REPS, assemble, 0)
    for one in others_in:
        one.wait()

    def own_block(k):
        return f_buf.at[1, turn(h, -k, NH), core]

    def own_in(k):
        here = own_block(k)
        behind = turn(h, -k, NH)
        arrived(here, "a_h", k, h_dev[k])
        send(here, f_buf.at[0, behind, core], "a_next", k, next_dev)
        send(here, f_buf.at[2, behind, core], "a_prev", k, prev_dev)
        send(here, here, "a_sib", k, sib_dev)

    def beside_in(k):
        before = f_buf.at[0, turn(h_prev, -k, NH), core]
        arrived(before, "a_next", k, prev_dev)
        send(before, before, "a_sib_prev", k, sib_dev)
        after = f_buf.at[2, turn(h_next, -k, NH), core]
        arrived(after, "a_prev", k, next_dev)
        send(after, after, "a_sib_next", k, sib_dev)

    def product(j, at, m):
        rows = pl.ds(pl.multiple_of(m * 256, 256), 256)
        return dot(a_mat[4 * j + at, rows, :], f_buf[j, at].reshape(256, FEAT)).reshape(2, TILE, FEAT)

    def add_own(*turns):
        places = [turn(h, -k, NH) for k in turns]
        for k, at in zip(turns, places):
            arrived(f_buf.at[1, at, other], "a_sib", k, sib_dev)

        def step(m, carry):
            part = product(1, places[0], m)
            for at in places[1:]:
                part = part + product(1, at, m)
            p_acc[m] = part if turns == (0,) else p_acc[m] + part
            return carry

        lax.fori_loop(0, NH, step, 0, unroll=True)

    def beside_at(k):
        before, after = turn(h_prev, -k, NH), turn(h_next, -k, NH)
        arrived(f_buf.at[0, before, other], "a_sib_prev", k, sib_dev)
        arrived(f_buf.at[2, after, other], "a_sib_next", k, sib_dev)
        return before, after

    def add_beside(k):
        before, after = beside_at(k)

        def step(m, carry):
            p_acc[m] = p_acc[m] + (product(0, before, m) + product(2, after, m))
            return carry

        lax.fori_loop(0, NH, step, 0, unroll=True)

    self_part = dot(feat_ref[...], ws_ref[...])
    own_in(1)
    own_in(3)
    beside_in(0)
    add_own(0)
    own_in(2)
    add_own(1, 3)
    beside_in(1)
    beside_in(3)
    add_beside(0)
    add_own(2)
    add_beside(1)
    beside_in(2)
    add_beside(3)

    before, after = beside_at(2)
    for k in (2, 1, 3, 0):
        m = turn(h, k, NH)
        p_acc[m] = p_acc[m] + (product(0, before, m) + product(2, after, m))
        c_send[k] = p_acc[m, other].astype(BF16)
        send(c_send.at[k], c_sib.at[k], "c_sib", k, sib_dev)
    for k in (2, 1, 3):
        arrived(c_sib.at[k], "c_sib", k, sib_dev)
        c_chip[k] = (p_acc[turn(h, k, NH), core] + c_sib[k].astype(F32)).astype(BF16)
        send(c_chip.at[k], c_recv.at[k], "c_h", k, h_dev[k])
    arrived(c_sib.at[0], "c_sib", 0, sib_dev)
    kernel_sum = p_acc[h, core] + c_sib[0].astype(F32)
    for k in (1, 3, 2):
        arrived(c_recv.at[k], "c_h", k, h_dev[k])
        kernel_sum = kernel_sum + c_recv[k].astype(F32)
    kernel_rows = kernel_sum.astype(BF16)

    preact = self_part + dot(kernel_rows, wk_ref[...])
    root = math.sqrt(2.0 / math.pi)
    square = preact * preact
    bend = jnp.tanh(root * (preact + 0.044715 * (square * preact)))
    half = 0.5 * (1.0 + bend)
    slope = half + 0.5 * preact * (1.0 - bend * bend) * (root * (1.0 + 3.0 * 0.044715 * square))
    grad_pre = (cot_ref[...].astype(F32) * slope).astype(BF16)

    g_t[h, core] = dot_nt(wk_ref[...], grad_pre).astype(BF16)
    mine = g_t.at[h, core]
    for k in (2, 1, 3):
        send(mine, mine, "e_h", k, h_dev[k])
    send(mine, mine, "e_sib", 0, sib_dev)
    out_ref[...] = (preact * half).astype(BF16)
    give(out_ref, out_hbm, 0)

    w_f32[0] = dot_tn(feat_ref[...], grad_pre)
    w_f32[1] = dot_tn(kernel_rows, grad_pre)
    w_send[...] = w_f32[other].astype(BF16)
    send(w_send, w_sib, "w_sib", 0, sib_dev)
    returned = dot_nt(ws_ref[...], grad_pre)

    def gradients(at):
        return jnp.concatenate([g_t[at, 0], g_t[at, 1]], axis=1)

    def back(at, left, n):
        rows = pl.ds(pl.multiple_of(at * 256, 256), 256)
        return dot(left, a_mat[n, rows, :])

    def add_back(*turns):
        places = [turn(h, -k, NH) for k in turns]
        for k, at in zip(turns, places):
            arrived(g_t.at[at, other], "e_sib", k, sib_dev)
        lefts = [gradients(at) for at in places]

        def step(n, carry):
            part = back(places[0], lefts[0], n)
            for at, left in zip(places[1:], lefts[1:]):
                part = part + back(at, left, n)
            r_acc[n] = part if turns == (0,) else r_acc[n] + part
            return carry

        lax.fori_loop(0, SPAN * NH, step, 0, unroll=True)

    def gradient_in(k):
        here = g_t.at[turn(h, -k, NH), core]
        arrived(here, "e_h", k, h_dev[k])
        send(here, here, "e_sib", k, sib_dev)

    def total(parts, count):
        one = parts[0].astype(F32)
        for q in range(1, count):
            one = one + parts[q].astype(F32)
        return one.astype(BF16)

    def chip_rows(block):
        rows = pl.ds(pl.multiple_of(block * 32, 32), 32)
        return w_f32[core, rows, :] + w_sib[rows, :].astype(F32)

    arrived(w_sib, "w_sib", 0, sib_dev)
    for k in range(1, NY):
        wy_send[k] = chip_rows(turn(y, k, NY)).astype(BF16)
        send(wy_send.at[k], wy_recv.at[k], "w_y", k, y_dev[k])
    add_back(0)
    gradient_in(1)
    gradient_in(3)
    add_back(1)
    gradient_in(2)

    for k in range(1, NY):
        arrived(wy_recv.at[k], "w_y", k, y_dev[k])
    part = chip_rows(y)
    for k in range(1, NY):
        part = part + wy_recv[k].astype(F32)
    wx_all[x] = part.astype(BF16)
    for k in range(1, NX):
        send(wx_all.at[x], wx_all.at[x], "w_x", k, x_dev[k])

    add_back(3)

    at = turn(h, -2, NH)
    arrived(g_t.at[at, other], "e_sib", 2, sib_dev)
    left = gradients(at)
    first_core = core == 0

    def products_back(j, base, k):
        q = turn(base, k, NH)
        part = r_acc[4 * j + q] + back(at, left, 4 * j + q)
        low, high = part[:, :TILE], part[:, TILE:]
        r_send[j, k] = jnp.where(first_core, high, low).astype(BF16)
        send(r_send.at[j, k], r_sib.at[j, k], "g_sib", 4 * j + k, sib_dev)
        r_own[j, k] = jnp.where(first_core, low, high)

    def to_beside(j, k, device):
        arrived(r_sib.at[j, k], "g_sib", 4 * j + k, sib_dev)
        r_chip[j // 2, k] = (r_own[j, k] + r_sib[j, k].astype(F32)).astype(BF16)
        send(r_chip.at[j // 2, k], r_l.at[j // 2, k], "g_l", 2 * j + k, device)

    def summed(k):
        arrived(r_sib.at[1, k], "g_sib", 4 + k, sib_dev)
        arrived(r_l.at[0, k], "g_l", k, next_dev)
        arrived(r_l.at[1, k], "g_l", 4 + k, prev_dev)
        return (r_own[1, k] + r_sib[1, k].astype(F32)) + (r_l[0, k].astype(F32) + r_l[1, k].astype(F32))

    def to_holder(k):
        r_hs[k] = summed(k).astype(BF16)
        send(r_hs.at[k], r_h.at[k], "g_h", k, h_dev[k])

    order = (2, 1, 3, 0)
    for step, k in enumerate(order):
        products_back(0, h_prev, k)
        products_back(2, h_next, k)
        if step > 0:
            to_beside(0, order[step - 1], prev_dev)
            to_beside(2, order[step - 1], next_dev)
    products_back(1, h, 2)
    to_beside(0, 0, prev_dev)
    to_beside(2, 0, next_dev)
    for q in range(1, NX):
        arrived(wx_all.at[turn(x, -q, NX)], "w_x", q, x_dev[q])
    wh_all[h] = total(wx_all, NX)
    for q in (2, 1, 3):
        send(wh_all.at[h], wh_all.at[h], "w_h", q, h_dev[q])
    for k in (1, 3, 0):
        products_back(1, h, k)

    for k in range(1, NH):
        arrived(wh_all.at[turn(h, -k, NH)], "w_h", k, h_dev[k])
    wl_all[l] = total(wh_all, NH)
    for k in range(1, NL):
        send(wl_all.at[l], wl_all.at[l], "w_l", k, l_dev[k])

    to_holder(2)

    for k in range(1, NL):
        arrived(wl_all.at[turn(l, -k, NL)], "w_l", k, l_dev[k])
    vy_all[y] = total(wl_all, NL)
    for k in range(1, NY):
        send(vy_all.at[y], vy_all.at[y], "v_y", k, y_dev[k])

    to_holder(1)
    to_holder(3)
    returned = returned + summed(0)

    settled = len(started) - 2 * NY
    for one in started[:settled]:
        one.wait_send()

    for k in (1, 3, 2):
        arrived(r_h.at[k], "g_h", k, h_dev[k])
        returned = returned + r_h[k].astype(F32)
    fg_ref[...] = returned.T.astype(BF16)
    give(fg_ref, fg_hbm, 1)

    for k in range(1, NY):
        arrived(vy_all.at[turn(y, -k, NY)], "v_y", k, y_dev[k])
    v_mat[core] = vy_all[...].reshape(FEAT, FEAT)
    send(v_mat.at[core], v_mat.at[core], "v_sib", 0, sib_dev)
    scale = 1.0 / math.sqrt(TILE * REPS * BANDS)
    wg_ref[core] = v_mat[core].astype(F32) * scale
    give(wg_ref.at[core], wg_hbm.at[core], 2)
    arrived(v_mat.at[other], "v_sib", 0, sib_dev)
    wg_ref[other] = v_mat[other].astype(F32) * scale
    give(wg_ref.at[other], wg_hbm.at[other], 3)

    for one in started[settled:]:
        one.wait_send()
    for one in given:
        one.wait()


def scratch():
    return [
        pltpu.VMEM((TILE, FEAT), BF16),
        pltpu.VMEM((TILE, FEAT), BF16),
        pltpu.VMEM((2, FEAT, FEAT), F32),
        pltpu.VMEM((TILE, FEAT), BF16),
        pltpu.VMEM((FEAT, FEAT), BF16),
        pltpu.VMEM((FEAT, FEAT), BF16),
        pltpu.VMEM((TILE, FEAT), BF16),
        pltpu.VMEM((2, 128), jnp.int32),
        pltpu.SMEM((2, 128), jnp.int32),
        pltpu.VMEM((SLOTS + 1, TILE, TILE), BF16),
        pltpu.VMEM((SPAN * NH, REPS * TILE, 2 * TILE), BF16),
        pltpu.VMEM((SPAN, NH, 2, TILE, FEAT), BF16),
        pltpu.VMEM((NH, 2, TILE, FEAT), F32),
        pltpu.VMEM((NH, TILE, FEAT), BF16),
        pltpu.VMEM((NH, TILE, FEAT), BF16),
        pltpu.VMEM((NH, TILE, FEAT), BF16),
        pltpu.VMEM((NH, TILE, FEAT), BF16),
        pltpu.VMEM((NH, 2, FEAT, TILE), BF16),
        pltpu.VMEM((SPAN * NH, FEAT, 2 * TILE), F32),
        pltpu.VMEM((SPAN, NH, FEAT, TILE), F32),
        pltpu.VMEM((SPAN, NH, FEAT, TILE), BF16),
        pltpu.VMEM((SPAN, NH, FEAT, TILE), BF16),
        pltpu.VMEM((2, NH, FEAT, TILE), BF16),
        pltpu.VMEM((2, NH, FEAT, TILE), BF16),
        pltpu.VMEM((NH, FEAT, TILE), BF16),
        pltpu.VMEM((NH, FEAT, TILE), BF16),
        pltpu.VMEM((2, FEAT, FEAT), F32),
        pltpu.VMEM((FEAT, FEAT), BF16),
        pltpu.VMEM((FEAT, FEAT), BF16),
        pltpu.VMEM((NY, 32, FEAT), BF16),
        pltpu.VMEM((NY, 32, FEAT), BF16),
        pltpu.VMEM((NX, 32, FEAT), BF16),
        pltpu.VMEM((NH, 32, FEAT), BF16),
        pltpu.VMEM((NL, 32, FEAT), BF16),
        pltpu.VMEM((NY, 32, FEAT), BF16),
        pltpu.VMEM((2, FEAT, FEAT), BF16),
        pltpu.SemaphoreType.DMA((13,)),
        pltpu.SemaphoreType.DMA((N_SEMS,)),
        pltpu.SemaphoreType.DMA((N_SEMS,)),
    ]


def hand_out(*refs):
    results, outputs, held, sem = refs[:3], refs[3:6], refs[6:9], refs[9]
    ins = [pltpu.make_async_copy(results[at], held[at], sem.at[at]) for at in range(3)]
    outs = [pltpu.make_async_copy(held[at], outputs[at], sem.at[3 + at]) for at in range(3)]
    for one in ins:
        one.start()
    for at in range(3):
        ins[at].wait()
        outs[at].start()
    for one in outs:
        one.wait()


def on_device(features, kernel_tiles, row_starts, column_block, self_weight, kernel_weight, cotangent):
    vmem = pl.BlockSpec(memory_space=pltpu.VMEM)
    hbm = pl.BlockSpec(memory_space=pltpu.HBM)
    shapes = (
        jax.ShapeDtypeStruct((TILE, FEAT), BF16),
        jax.ShapeDtypeStruct((TILE, FEAT), BF16),
        jax.ShapeDtypeStruct((2, FEAT, FEAT), F32),
    )
    results = pl.pallas_call(
        kernel,
        out_shape=shapes,
        in_specs=[pl.BlockSpec(memory_space=pltpu.SMEM), vmem, hbm, hbm, hbm, hbm, hbm],
        out_specs=(pl.BlockSpec(memory_space=pl.ANY),) * 3,
        scratch_shapes=scratch(),
        compiler_params=pltpu.CompilerParams(
            collective_id=0, has_side_effects=True, vmem_limit_bytes=64 * 1024 * 1024 - 65536
        ),
    )(row_starts, column_block, features, self_weight, kernel_weight, cotangent, kernel_tiles)
    return pl.pallas_call(
        hand_out,
        out_shape=shapes,
        in_specs=[pl.BlockSpec(memory_space=pl.ANY)] * 3,
        out_specs=(pl.BlockSpec(memory_space=pl.ANY),) * 3,
        scratch_shapes=[pltpu.VMEM(one.shape, one.dtype) for one in shapes] + [pltpu.SemaphoreType.DMA((6,))],
        compiler_params=pltpu.CompilerParams(vmem_limit_bytes=64 * 1024 * 1024 - 65536),
    )(*results)


def solution(mesh):
    split = P(("loop", "rep"), None)
    return jax.shard_map(
        on_device,
        mesh=mesh,
        in_specs=(split, P(("loop", "rep"), None, None, None), split, split, P(), P(), split),
        out_specs=(split, split, P()),
        check_vma=False,
    )
```
